128 devices in a mesh: ctx: 8 (over y, z_lo), head: 16 (over z_hi, x, core).
Axes of the slice: x: 4, y: 4, z: 4 (z_hi: 2, z_lo: 2; z = z_hi * 2 + z_lo), core: 2. Of those that a mesh axis runs over, the one named last changes fastest.
Arguments:
- q_nope: bfloat16 [2048, 16384], P('ctx', 'head'), may hold values from -6 to 6
- q_rope: bfloat16 [2048, 8192], P('ctx', 'head'), may hold values from -6 to 6
- grad_out: bfloat16 [2048, 16384], P('ctx', 'head'), may hold values from -6 to 6
- kv_latent: bfloat16 [2048, 576], P('ctx'), may hold values from -6 to 6
- w_uk: bfloat16 [512, 16384], P(None, 'head'), may hold values from -0.5 to 0.5
- w_uv: bfloat16 [512, 16384], P(None, 'head'), may hold values from -0.25 to 0.25
- group_order: int32 [16], replicated, may hold values from 0 to 15, each once
Outputs:
- grad_q_nope: bfloat16 [2048, 16384], P('ctx', 'head')
- grad_q_rope: bfloat16 [2048, 8192], P('ctx', 'head')
- grad_kv: bfloat16 [2048, 576], P('ctx')
- grad_w_uk: float32 [512, 16384], P(None, 'head')
- grad_w_uv: float32 [512, 16384], P(None, 'head')
The draws below stay inside these ranges and needn't reach their ends.
Inputs may be any that keep to these rules, and one draw needn't show every extreme that they name: `group_order`: each of the 16 sequence blocks appears once.
All inputs are finite; a program needn't handle non-finite values.
Results may differ from the reference program's by a relative error of at most 0.017.
Values may be sent and summed in bfloat16 or wider, within the bound.
No kernel may reach another device: no remote copies, remote signals or barrier semaphores. Data moves between devices by JAX's collectives and lax.ppermute only.
A program may use at most 64 MiB of HBM per device.

```python
import math
import jax
import jax.numpy as jnp
from jax import lax

HEADS = 128
NOPE = 128
ROPE = 64
VHEAD = 128
LATENT = 512
GROUP = 128
GROUPS = 16
TOKENS = 2048


def draw_q_rope(key, part):
    key = jax.random.fold_in(key, 11)
    first = jax.random.fold_in(key, 0)
    full = jnp.clip(jax.random.normal(first, (TOKENS, HEADS, ROPE), jnp.float32), -6.0, 6.0)
    return full.reshape(TOKENS, HEADS * ROPE).astype(jnp.bfloat16)


def draw_kv_latent(key, part):
    key = jax.random.fold_in(key, 23)
    first, second = jax.random.split(key, 2)
    latent = 0.4 * jnp.clip(jax.random.normal(first, (TOKENS, LATENT), jnp.float32), -6.0, 6.0)
    rotary = jnp.clip(jax.random.normal(second, (TOKENS, ROPE), jnp.float32), -6.0, 6.0)
    return jnp.concatenate([latent, rotary], axis=1).astype(jnp.bfloat16)


def block_levels(key, extent, cuts, smallest, top_value):
    level = 1.0
    for position, parts in cuts:
        steps = jax.random.uniform(jax.random.fold_in(jax.random.fold_in(key, 6), position), (parts,), jnp.float32, smallest / len(cuts), top_value / len(cuts))
        level = level * jnp.repeat(jnp.exp(steps), extent[position] // parts).reshape((-1,) + (1,) * (len(extent) - 1 - position))
    return level


def bell_draw(rng, dims, spread, bound, pieces=(), kind=jnp.bfloat16):
    entries = spread * jax.random.normal(rng, dims, jnp.float32)
    if pieces:
        entries = entries * block_levels(rng, dims, pieces, -0.22, 0.18)
    return jnp.clip(entries, -bound, bound).astype(kind)


def setup_inputs(seed: int = 0) -> dict:
    splits = jax.random.split(jax.random.key(seed), 8)
    return {
        "q_nope": bell_draw(splits[0], (TOKENS, HEADS * NOPE), 1.0, 6.0, ((0, 8), (1, 16))),
        "q_rope": draw_q_rope(jax.random.fold_in(splits[7], 71), 0),
        "grad_out": bell_draw(splits[2], (TOKENS, HEADS * VHEAD), 1.0, 6.0, ((0, 8), (1, 16))),
        "kv_latent": draw_kv_latent(jax.random.fold_in(splits[7], 71), 0),
        "w_uk": bell_draw(splits[4], (LATENT, HEADS * NOPE), NOPE ** -0.5, 0.5, ((1, 16),)),
        "w_uv": bell_draw(splits[5], (LATENT, HEADS * VHEAD), LATENT ** -0.5, 0.25, ((1, 16),)),
        "group_order": jax.random.permutation(splits[6], GROUPS).astype(jnp.int32),
    }


def one_head(kv_latent, visible, scale, q_h, r_h, g_h, uk_h, uv_h):
    values = kv_latent[:, :LATENT]
    qa = jnp.dot(q_h, uk_h.T, preferred_element_type=jnp.float32).astype(jnp.bfloat16)
    q_full = jnp.concatenate([qa, r_h], axis=1)
    scores = jnp.dot(q_full, kv_latent.T, preferred_element_type=jnp.float32) * scale
    scores = jnp.where(visible, scores, -jnp.inf)
    top = jnp.max(scores, axis=1, keepdims=True)
    expo = jnp.exp(scores - top)
    probs = expo / jnp.sum(expo, axis=1, keepdims=True)
    probs_b = probs.astype(jnp.bfloat16)
    out_lat = jnp.dot(probs_b, values, preferred_element_type=jnp.float32).astype(jnp.bfloat16)
    grad_lat = jnp.dot(g_h, uv_h.T, preferred_element_type=jnp.float32).astype(jnp.bfloat16)
    grad_probs = jnp.dot(grad_lat, values.T, preferred_element_type=jnp.float32)
    delta = jnp.sum(probs * grad_probs, axis=1, keepdims=True)
    grad_scores = (scale * probs * (grad_probs - delta)).astype(jnp.bfloat16)
    grad_qfull = jnp.dot(grad_scores, kv_latent, preferred_element_type=jnp.float32)
    grad_qa = grad_qfull[:, :LATENT].astype(jnp.bfloat16)
    grad_rope = grad_qfull[:, LATENT:].astype(jnp.bfloat16)
    grad_nope = jnp.dot(grad_qa, uk_h, preferred_element_type=jnp.float32).astype(jnp.bfloat16)
    grad_wuk = jnp.dot(grad_qa.T, q_h, preferred_element_type=jnp.float32)
    grad_wuv = jnp.dot(out_lat.T, g_h, preferred_element_type=jnp.float32)
    score_part = jnp.dot(grad_scores.T, q_full, preferred_element_type=jnp.float32)
    value_part = jnp.dot(probs_b.T, grad_lat, preferred_element_type=jnp.float32)
    grad_keys = score_part + jnp.pad(value_part, ((0, 0), (0, ROPE)))
    return grad_keys, (grad_nope, grad_rope, grad_wuk, grad_wuv)


def by_heads(array, width):
    return array.reshape(array.shape[0], HEADS, width).transpose(1, 0, 2)


def reference(q_nope, q_rope, grad_out, kv_latent, w_uk, w_uv, group_order):
    mscale = 0.1 * math.log(40.0) + 1.0
    scale = (NOPE + ROPE) ** -0.5 * mscale * mscale
    rows = jnp.arange(TOKENS, dtype=jnp.int32)
    pos = group_order[rows // GROUP].astype(jnp.int32) * GROUP + rows % GROUP
    visible = pos[:, None] >= pos[None, :]

    def step(carry, items):
        grad_keys, outs = one_head(kv_latent, visible, scale, *items)
        return carry + grad_keys, outs

    items = (by_heads(q_nope, NOPE), by_heads(q_rope, ROPE), by_heads(grad_out, VHEAD),
             by_heads(w_uk, NOPE), by_heads(w_uv, VHEAD))
    total, (g_nope, g_rope, g_uk, g_uv) = lax.scan(step, jnp.zeros((TOKENS, LATENT + ROPE), jnp.float32), items)
    grad_q_nope = g_nope.transpose(1, 0, 2).reshape(TOKENS, HEADS * NOPE)
    grad_q_rope = g_rope.transpose(1, 0, 2).reshape(TOKENS, HEADS * ROPE)
    grad_w_uk = g_uk.transpose(1, 0, 2).reshape(LATENT, HEADS * NOPE)
    grad_w_uv = g_uv.transpose(1, 0, 2).reshape(LATENT, HEADS * VHEAD)
    return grad_q_nope, grad_q_rope, total.astype(jnp.bfloat16), grad_w_uk, grad_w_uv
```

```python
import functools
import math

import jax
import jax.numpy as jnp
from jax import lax
from jax.experimental import pallas as pl
from jax.experimental.pallas import tpu as pltpu
from jax.sharding import PartitionSpec as P

NOPE = 128
ROPE = 64
VHEAD = 128
LATENT = 512
GROUP = 128
GROUPS = 16
TOKENS = GROUP * GROUPS
CTX = 8
HEAD = 16
MSCALE = 0.1 * math.log(40.0) + 1.0
SCALE = (NOPE + ROPE) ** (-0.5) * MSCALE * MSCALE
BLOCK = 256
F32 = jnp.float32
BF16 = jnp.bfloat16
VMEM = pl.BlockSpec(memory_space=pltpu.VMEM)
SMEM = pl.BlockSpec(memory_space=pltpu.SMEM)
PARAMS = pltpu.CompilerParams(vmem_limit_bytes=56 * 1024 * 1024)

Q0, G0, R0, K0, KR0, CHUNK = 0, 256, 512, 640, 1152, 1216


def nt(a, b):
    return lax.dot_general(a, b, (((1,), (1,)), ((), ())), preferred_element_type=F32)


def nn(a, b):
    return jnp.dot(a, b, preferred_element_type=F32)


def pack_kernel(core, q, r, g, kv, send):
    half = kv[pl.ds(pl.multiple_of(core[0] * GROUP, GROUP), GROUP), :]
    for i in range(CTX):
        send[i, Q0:Q0 + 256, :] = q[:, i * 128:(i + 1) * 128]
        send[i, G0:G0 + 256, :] = g[:, i * 128:(i + 1) * 128]
        rope = r[:, i * ROPE:(i + 1) * ROPE]
        send[i, R0:R0 + 128, :] = jnp.concatenate([rope[:128], rope[128:]], axis=1)
        for j in range(4):
            send[i, K0 + 128 * j:K0 + 128 * (j + 1), :] = half[:, 128 * j:128 * (j + 1)]
        tail = half[:, LATENT:]
        send[i, KR0:KR0 + 64, :] = jnp.concatenate([tail[:64], tail[64:]], axis=1)


def pack(core, q, r, g, kv):
    return pl.pallas_call(
        pack_kernel,
        out_shape=jax.ShapeDtypeStruct((CTX, CHUNK, 128), BF16),
        in_specs=[SMEM, VMEM, VMEM, VMEM, VMEM],
        out_specs=VMEM,
        compiler_params=PARAMS,
        name="pack",
    )(core, q, r, g, kv)


def head_kernel(order, core, recv, other, uk, uv, send, guk, guv,
                val, qf, go, kf, kt, vf, gk, gv, gq):
    def gather(p, carry):
        s = order[p]
        c, b = s // 2, s % 2
        rows = pl.ds(pl.multiple_of(p * GROUP, GROUP), GROUP)
        shift = pl.multiple_of(b * GROUP, GROUP)
        qf[rows, :NOPE] = recv[c, pl.ds(Q0 + shift, GROUP), :]
        go[rows, :] = recv[c, pl.ds(G0 + shift, GROUP), :]
        pair = recv[c, R0:R0 + 128, :]
        qf[rows, NOPE:] = jnp.where(b == 0, pair[:, :ROPE], pair[:, ROPE:])

        def take(ref, base):
            for j in range(4):
                val[rows, 128 * j:128 * (j + 1)] = ref[c, base + 128 * j:base + 128 * (j + 1), :]
            tail = ref[c, base + 512:base + 576, :]
            kf[rows, NOPE:] = jnp.concatenate([tail[:, :ROPE], tail[:, ROPE:]], axis=0)

        @pl.when(b == core[0])
        def _():
            take(recv, K0)

        @pl.when(b != core[0])
        def _():
            take(other, 0)

        return carry

    lax.fori_loop(0, GROUPS, gather, 0)

    ukt = jnp.transpose(uk[...].astype(F32)).astype(BF16)
    for p in range(TOKENS // BLOCK):
        rows = slice(p * BLOCK, (p + 1) * BLOCK)
        latent = val[rows, :]
        kf[rows, :NOPE] = nn(latent, uk[...]).astype(BF16)
        vf[rows, :] = nn(latent, uv[...]).astype(BF16)
        kt[:NOPE, rows] = nt(ukt, latent).astype(BF16)
        kt[NOPE:, rows] = jnp.transpose(kf[rows, NOPE:].astype(F32)).astype(BF16)

    factor = SCALE * math.log2(math.e)
    key_at = lax.broadcasted_iota(jnp.int32, (BLOCK, BLOCK), 0)
    query_at = lax.broadcasted_iota(jnp.int32, (BLOCK, BLOCK), 1)
    seen = key_at <= query_at
    for i in range(TOKENS // BLOCK):
        mine = slice(i * BLOCK, (i + 1) * BLOCK)
        q_i, g_i = qf[mine, :], go[mine, :]
        scores = []
        for j in range(i + 1):
            s = nt(kf[j * BLOCK:(j + 1) * BLOCK, :], q_i) * factor
            if j == i:
                s = jnp.where(seen, s, -jnp.inf)
            scores.append(s)
        top = functools.reduce(jnp.maximum, [jnp.max(s, axis=0, keepdims=True) for s in scores])
        expo = [jnp.exp2(s - top) for s in scores]
        total = functools.reduce(jnp.add, [jnp.sum(e, axis=0, keepdims=True) for e in expo])
        inverse = 1.0 / total
        grads = [nt(vf[j * BLOCK:(j + 1) * BLOCK, :], g_i) for j in range(i + 1)]
        delta = functools.reduce(
            jnp.add, [jnp.sum(e * d, axis=0, keepdims=True) for e, d in zip(expo, grads)]
        ) * inverse
        acc = None
        for j in range(i + 1):
            rows = slice(j * BLOCK, (j + 1) * BLOCK)
            probs = expo[j] * inverse
            ds = (probs * (grads[j] - delta)).astype(BF16)
            part = nn(kt[:, rows], ds)
            acc = part if acc is None else acc + part
            to_k = nn(ds, q_i)
            to_v = nn(probs.astype(BF16), g_i)
            if j == i:
                gk[rows, :] = to_k
                gv[rows, :] = to_v
            else:
                gk[rows, :] += to_k
                gv[rows, :] += to_v
        gq[mine, :] = jnp.transpose(acc) * SCALE

    uk_sum = uv_sum = None
    for p in range(TOKENS // BLOCK):
        rows = slice(p * BLOCK, (p + 1) * BLOCK)
        latent = val[rows, :]
        kp = nn(jnp.transpose(gk[rows, :NOPE] * SCALE).astype(BF16), latent)
        vp = nn(jnp.transpose(gv[rows, :]).astype(BF16), latent)
        uk_sum = kp if uk_sum is None else uk_sum + kp
        uv_sum = vp if uv_sum is None else uv_sum + vp
    guk[...] = jnp.transpose(uk_sum).astype(BF16)
    guv[...] = jnp.transpose(uv_sum).astype(BF16)

    def scatter(p, carry):
        s = order[p]
        c, b = s // 2, s % 2
        rows = pl.ds(pl.multiple_of(p * GROUP, GROUP), GROUP)
        to = pl.ds(pl.multiple_of(b * GROUP, GROUP), GROUP)
        send[c, to, :128] = gq[rows, :NOPE].astype(BF16)
        send[c, to, 128:256] = (gk[rows, :NOPE] * SCALE).astype(BF16)
        send[c, to, 256:384] = gv[rows, :].astype(BF16)
        send[c, to, 384:512] = jnp.concatenate(
            [gq[rows, NOPE:], gk[rows, NOPE:] * SCALE], axis=1
        ).astype(BF16)
        return carry

    lax.fori_loop(0, GROUPS, scatter, 0)


def head_call(order, core, recv, other, uk, uv):
    return pl.pallas_call(
        head_kernel,
        out_shape=(
            jax.ShapeDtypeStruct((CTX, 256, 512), BF16),
            jax.ShapeDtypeStruct((LATENT, NOPE), BF16),
            jax.ShapeDtypeStruct((LATENT, VHEAD), BF16),
        ),
        in_specs=[SMEM, SMEM, VMEM, VMEM, VMEM, VMEM],
        out_specs=(VMEM, VMEM, VMEM),
        scratch_shapes=[
            pltpu.VMEM((TOKENS, LATENT), BF16),
            pltpu.VMEM((TOKENS, NOPE + ROPE), BF16),
            pltpu.VMEM((TOKENS, VHEAD), BF16),
            pltpu.VMEM((TOKENS, NOPE + ROPE), BF16),
            pltpu.VMEM((NOPE + ROPE, TOKENS), BF16),
            pltpu.VMEM((TOKENS, VHEAD), BF16),
            pltpu.VMEM((TOKENS, NOPE + ROPE), F32),
            pltpu.VMEM((TOKENS, VHEAD), F32),
            pltpu.VMEM((TOKENS, NOPE + ROPE), F32),
        ],
        compiler_params=PARAMS,
        name="head",
    )(order, core, recv, other, uk, uv)


def post_kernel(core, back, uk, uv, gqn, gqr, own, away):
    acc = None
    rope = None
    for i in range(CTX):
        cols = slice(i * 128, (i + 1) * 128)
        gqn[:, cols] = back[i, :, :128]
        gqr[:, i * ROPE:(i + 1) * ROPE] = back[i, :, 384:448]
        part = nt(back[i, :, 128:256], uk[:, cols]) + nt(back[i, :, 256:384], uv[:, cols])
        tail = back[i, :, 448:].astype(F32)
        acc = part if acc is None else acc + part
        rope = tail if rope is None else rope + tail
    low = core[0] == 0
    own[:, :LATENT] = jnp.where(low, acc[:128], acc[128:])
    own[:, LATENT:] = jnp.where(low, rope[:128], rope[128:])
    away[:, :LATENT] = jnp.where(low, acc[128:], acc[:128]).astype(BF16)
    away[:, LATENT:] = jnp.where(low, rope[128:], rope[:128]).astype(BF16)


def post(core, back, uk, uv):
    width = LATENT + ROPE
    return pl.pallas_call(
        post_kernel,
        out_shape=(
            jax.ShapeDtypeStruct((256, 1024), BF16),
            jax.ShapeDtypeStruct((256, 512), BF16),
            jax.ShapeDtypeStruct((128, width), F32),
            jax.ShapeDtypeStruct((128, width), BF16),
        ),
        in_specs=[SMEM, VMEM, VMEM, VMEM],
        out_specs=(VMEM, VMEM, VMEM, VMEM),
        compiler_params=PARAMS,
        name="post",
    )(core, back, uk, uv)


def spread(array, axis, groups=None, count=CTX):
    copies = jnp.broadcast_to(array[None], (count,) + array.shape)
    return lax.all_to_all(copies, axis, 0, 0, tiled=True, axis_index_groups=groups)


def on_device(q_nope, q_rope, grad_out, kv_latent, w_uk, w_uv, group_order):
    slots = jnp.arange(GROUPS, dtype=jnp.int32)
    order = jnp.sum(jnp.where(group_order[None, :] == slots[:, None], slots[None, :], 0), axis=1)
    mine = lax.axis_index("ctx")
    core = (lax.axis_index("head") % 2).astype(jnp.int32)[None]
    swap = [(i, i ^ 1) for i in range(HEAD)]
    lanes = [[c + 2 * k for k in range(CTX)] for c in range(2)]

    sent = pack(core, q_nope, q_rope, grad_out, kv_latent)
    recv = lax.all_to_all(sent, "ctx", 0, 0, tiled=True)
    other = lax.ppermute(recv[:, K0:, :], "head", swap)
    uk_h = lax.dynamic_slice_in_dim(w_uk, mine * NOPE, NOPE, 1)
    uv_h = lax.dynamic_slice_in_dim(w_uv, mine * VHEAD, VHEAD, 1)
    back, guk, guv = head_call(order, core, recv, other, uk_h, uv_h)
    back = lax.all_to_all(back, "ctx", 0, 0, tiled=True)
    grads = spread(jnp.concatenate([guk, guv], axis=0), "ctx")
    gqn, gqr, own, away = post(core, back, w_uk, w_uv)
    pair = (own + lax.ppermute(away, "head", swap).astype(F32)).astype(BF16)
    total = jnp.sum(spread(pair, "head", lanes).astype(F32), axis=0).astype(BF16)
    peer = lax.ppermute(total, "head", swap)
    low = core[0] == 0
    grad_kv = jnp.concatenate(
        [jnp.where(low, total, peer), jnp.where(low, peer, total)], axis=0
    )
    wide = grads.astype(F32)
    sum_uk = wide[:, :LATENT].transpose(1, 0, 2).reshape(LATENT, CTX * NOPE)
    sum_uv = wide[:, LATENT:].transpose(1, 0, 2).reshape(LATENT, CTX * VHEAD)
    return gqn, gqr, grad_kv, sum_uk, sum_uv


def solution(mesh):
    in_specs = (
        P("ctx", "head"),
        P("ctx", "head"),
        P("ctx", "head"),
        P("ctx", None),
        P(None, "head"),
        P(None, "head"),
        P(),
    )
    out_specs = (
        P("ctx", "head"),
        P("ctx", "head"),
        P("ctx", None),
        P(None, "head"),
        P(None, "head"),
    )
    return jax.shard_map(
        on_device, mesh=mesh, in_specs=in_specs, out_specs=out_specs, check_vma=False
    )
```

```python
import functools
import math

import jax
import jax.numpy as jnp
from jax import lax
from jax.experimental import pallas as pl
from jax.experimental.pallas import tpu as pltpu
from jax.sharding import PartitionSpec as P

NOPE = 128
ROPE = 64
VHEAD = 128
LATENT = 512
WIDTH = LATENT + ROPE
GROUP = 128
GROUPS = 16
TOKENS = GROUP * GROUPS
CTX = 8
HEAD = 16
MSCALE = 0.1 * math.log(40.0) + 1.0
SCALE = (NOPE + ROPE) ** (-0.5) * MSCALE * MSCALE
BLOCK = 256
BLOCKS = TOKENS // BLOCK
F32 = jnp.float32
BF16 = jnp.bfloat16
VMEM = pl.BlockSpec(memory_space=pltpu.VMEM)
SMEM = pl.BlockSpec(memory_space=pltpu.SMEM)
PARAMS = pltpu.CompilerParams(vmem_limit_bytes=56 * 1024 * 1024)


def nt(a, b):
    return lax.dot_general(a, b, (((1,), (1,)), ((), ())), preferred_element_type=F32)


def nn(a, b):
    return jnp.dot(a, b, preferred_element_type=F32)


def pack_kernel(q, r, g, send):
    for i in range(CTX):
        send[i, :256, :] = q[:, i * 128:(i + 1) * 128]
        send[i, 256:512, :] = g[:, i * 128:(i + 1) * 128]
        rope = r[:, i * ROPE:(i + 1) * ROPE]
        send[i, 512:, :] = jnp.concatenate([rope[:128], rope[128:]], axis=1)


def pack(q, r, g):
    return pl.pallas_call(
        pack_kernel,
        out_shape=jax.ShapeDtypeStruct((CTX, 640, 128), BF16),
        in_specs=[VMEM, VMEM, VMEM],
        out_specs=VMEM,
        compiler_params=PARAMS,
        name="pack",
    )(q, r, g)


def head_kernel(order, place, recv, *refs):
    latents, (uk, uv, keys, rest, val, qf, go, kf, kt, vf, gk, gv, gq) = refs[:8], refs[8:]
    me, core = place[0], place[1]
    y, z = me // 2, lax.rem(me, 2)

    def at(s):
        return pl.ds(pl.multiple_of(order[s] * GROUP, GROUP), GROUP)

    for dy in range(4):
        for rc in range(2):
            for rz in range(2):
                c = lax.rem(y + dy, 4) * 2 + lax.rem(z + rz, 2)
                cols = at(c * 2 + lax.rem(core + rc, 2))
                src = latents[dy * 2 + rc]
                val[:, cols] = src[rz, :LATENT, :]
                kt[NOPE:, cols] = src[rz, LATENT:, :]
    for s in range(GROUPS):
        c, b = s // 2, s % 2
        rows = at(s)
        qf[rows, :NOPE] = recv[c, b * 128:(b + 1) * 128, :]
        go[rows, :] = recv[c, 256 + b * 128:256 + (b + 1) * 128, :]
        qf[rows, NOPE:] = recv[c, 512:640, b * ROPE:(b + 1) * ROPE]

    ukt = jnp.transpose(uk[...].astype(F32)).astype(BF16)
    uvt = jnp.transpose(uv[...].astype(F32)).astype(BF16)
    for p in range(BLOCKS):
        rows = slice(p * BLOCK, (p + 1) * BLOCK)
        latent = val[:, rows]
        k_t = nn(ukt, latent)
        kt[:NOPE, rows] = k_t.astype(BF16)
        kf[rows, :NOPE] = jnp.transpose(k_t).astype(BF16)
        kf[rows, NOPE:] = jnp.transpose(kt[NOPE:, rows].astype(F32)).astype(BF16)
        vf[rows, :] = jnp.transpose(nn(uvt, latent)).astype(BF16)

    factor = SCALE * math.log2(math.e)
    key_at = lax.broadcasted_iota(jnp.int32, (BLOCK, BLOCK), 0)
    query_at = lax.broadcasted_iota(jnp.int32, (BLOCK, BLOCK), 1)
    seen = key_at <= query_at
    for i in range(BLOCKS):
        mine = slice(i * BLOCK, (i + 1) * BLOCK)
        q_i, g_i = qf[mine, :], go[mine, :]
        scores = []
        for j in range(i + 1):
            s = nt(kf[j * BLOCK:(j + 1) * BLOCK, :], q_i) * factor
            if j == i:
                s = jnp.where(seen, s, -jnp.inf)
            scores.append(s)
        top = functools.reduce(jnp.maximum, [jnp.max(s, axis=0, keepdims=True) for s in scores])
        expo = [jnp.exp2(s - top) for s in scores]
        total = functools.reduce(jnp.add, [jnp.sum(e, axis=0, keepdims=True) for e in expo])
        inverse = 1.0 / total
        grads = [nt(vf[j * BLOCK:(j + 1) * BLOCK, :], g_i) for j in range(i + 1)]
        delta = functools.reduce(
            jnp.add, [jnp.sum(e * d, axis=0, keepdims=True) for e, d in zip(expo, grads)]
        ) * inverse
        acc = None
        for j in range(i + 1):
            rows = slice(j * BLOCK, (j + 1) * BLOCK)
            probs = expo[j] * inverse
            ds = (probs * (grads[j] - delta)).astype(BF16)
            part = nn(kt[:, rows], ds)
            acc = part if acc is None else acc + part
            to_k = nn(ds, q_i)
            to_v = nn(probs.astype(BF16), g_i)
            if j == i:
                gk[rows, :] = to_k
                gv[rows, :] = to_v
            else:
                gk[rows, :] += to_k
                gv[rows, :] += to_v
        gq[mine, :] = jnp.transpose(acc) * SCALE

    gkb = (gk[...] * SCALE).astype(BF16)
    gvb = gv[...].astype(BF16)
    guk = nn(val[...], gkb[:, :NOPE]).astype(BF16)
    guv = nn(val[...], gvb).astype(BF16)
    kf[...] = gkb
    vf[...] = gvb
    for c in range(CTX):
        rest[c, 384:896, :] = guk
        rest[c, 896:, :] = guv
        lo, hi = at(2 * c), at(2 * c + 1)
        keys[c, :128, :] = kf[lo, :NOPE]
        keys[c, 128:256, :] = kf[hi, :NOPE]
        keys[c, 256:384, :] = vf[lo, :]
        keys[c, 384:512, :] = vf[hi, :]
        keys[c, 512:, :] = jnp.concatenate([kf[lo, NOPE:], kf[hi, NOPE:]], axis=1)
        first, second = gq[lo, :], gq[hi, :]
        rest[c, :128, :] = first[:, :NOPE].astype(BF16)
        rest[c, 128:256, :] = second[:, :NOPE].astype(BF16)
        rest[c, 256:384, :] = jnp.concatenate(
            [first[:, NOPE:], second[:, NOPE:]], axis=1
        ).astype(BF16)


def head_call(order, place, recv, latents, uk, uv):
    whole = lambda shape: pl.BlockSpec(shape, lambda t, o, m: (0,) * len(shape))
    column = pl.BlockSpec((LATENT, NOPE), lambda t, o, m: (0, m[0]))
    return pl.pallas_call(
        head_kernel,
        out_shape=(
            jax.ShapeDtypeStruct((CTX, 640, 128), BF16),
            jax.ShapeDtypeStruct((CTX, 1408, 128), BF16),
        ),
        grid_spec=pltpu.PrefetchScalarGridSpec(
            num_scalar_prefetch=2,
            grid=(1,),
            in_specs=[whole((CTX, 640, 128))] + [whole((2, WIDTH, 128))] * 8 + [column, column],
            out_specs=(whole((CTX, 640, 128)), whole((CTX, 1408, 128))),
            scratch_shapes=[
                pltpu.VMEM((LATENT, TOKENS), BF16),
                pltpu.VMEM((TOKENS, NOPE + ROPE), BF16),
                pltpu.VMEM((TOKENS, VHEAD), BF16),
                pltpu.VMEM((TOKENS, NOPE + ROPE), BF16),
                pltpu.VMEM((NOPE + ROPE, TOKENS), BF16),
                pltpu.VMEM((TOKENS, VHEAD), BF16),
                pltpu.VMEM((TOKENS, NOPE + ROPE), F32),
                pltpu.VMEM((TOKENS, VHEAD), F32),
                pltpu.VMEM((TOKENS, NOPE + ROPE), F32),
            ],
        ),
        compiler_params=PARAMS,
        name="head",
    )(order, place, recv, *latents, uk, uv)


def post_kernel(place, back, uk, uv, own, away):
    acc = rope = None
    for i in range(CTX):
        cols = slice(i * 128, (i + 1) * 128)
        part = nt(uk[:, cols], back[i, :256, :]) + nt(uv[:, cols], back[i, 256:512, :])
        tail = back[i, 512:, :].astype(F32)
        acc = part if acc is None else acc + part
        rope = tail if rope is None else rope + tail
    turned = jnp.transpose(rope)
    low = place[1] == 0
    own[:LATENT, :] = jnp.where(low, acc[:, :128], acc[:, 128:])
    own[LATENT:, :] = jnp.where(low, turned[:ROPE], turned[ROPE:])
    away[:LATENT, :] = jnp.where(low, acc[:, 128:], acc[:, :128]).astype(BF16)
    away[LATENT:, :] = jnp.where(low, turned[ROPE:], turned[:ROPE]).astype(BF16)


def post(place, back, uk, uv):
    return pl.pallas_call(
        post_kernel,
        out_shape=(
            jax.ShapeDtypeStruct((WIDTH, 128), F32),
            jax.ShapeDtypeStruct((WIDTH, 128), BF16),
        ),
        in_specs=[SMEM, VMEM, VMEM, VMEM],
        out_specs=(VMEM, VMEM),
        compiler_params=PARAMS,
        name="post",
    )(place, back, uk, uv)


def finish_kernel(rest, gqn, gqr, guk, guv):
    for t in range(2):
        cols = slice(128 * t, 128 * (t + 1))
        gqn[:, cols] = rest[t, :256, :]
        pair = rest[t, 256:384, :]
        gqr[:128, ROPE * t:ROPE * (t + 1)] = pair[:, :ROPE]
        gqr[128:, ROPE * t:ROPE * (t + 1)] = pair[:, ROPE:]
        guk[:, cols] = rest[t, 384:896, :].astype(F32)
        guv[:, cols] = rest[t, 896:, :].astype(F32)


def finish(rest):
    return pl.pallas_call(
        finish_kernel,
        out_shape=(
            jax.ShapeDtypeStruct((256, 1024), BF16),
            jax.ShapeDtypeStruct((256, 512), BF16),
            jax.ShapeDtypeStruct((LATENT, 1024), F32),
            jax.ShapeDtypeStruct((LATENT, 1024), F32),
        ),
        grid=(4,),
        in_specs=[pl.BlockSpec((2, 1408, 128), lambda t: (t, 0, 0))],
        out_specs=(
            pl.BlockSpec((256, 256), lambda t: (0, t)),
            pl.BlockSpec((256, 128), lambda t: (0, t)),
            pl.BlockSpec((LATENT, 256), lambda t: (0, t)),
            pl.BlockSpec((LATENT, 256), lambda t: (0, t)),
        ),
        compiler_params=PARAMS,
        name="finish",
    )(rest)


CORE_SWAP = [(i, i ^ 1) for i in range(HEAD)]
ZLO_SWAP = [(i, i ^ 1) for i in range(CTX)]
ZHI_SWAP = [(i, i ^ 8) for i in range(HEAD)]


def from_y(step):
    return [(((c // 2 + step) % 4) * 2 + c % 2, c) for c in range(CTX)]


def from_x(step):
    return [((h & 8) + ((h // 2 + step) % 4) * 2 + h % 2, h) for h in range(HEAD)]


def gather_latent(half):
    near = jnp.stack([half, lax.ppermute(half, "ctx", ZLO_SWAP)])
    found = [near] + [lax.ppermute(near, "ctx", from_y(d)) for d in (1, 2, 3)]
    return [part for f in found for part in (f, lax.ppermute(f, "head", CORE_SWAP))]


def sum_heads(own, away):
    pair = (own + lax.ppermute(away, "head", CORE_SWAP).astype(F32)).astype(BF16)
    one, two, three = (lax.ppermute(pair, "head", from_x(d)).astype(F32) for d in (1, 2, 3))
    quad = ((pair.astype(F32) + two) + (one + three)).astype(BF16)
    far = lax.ppermute(quad, "head", ZHI_SWAP)
    return (quad.astype(F32) + far.astype(F32)).astype(BF16)


def on_device(q_nope, q_rope, grad_out, kv_latent, w_uk, w_uv, group_order):
    core = lax.axis_index("head") % 2
    place = jnp.stack([lax.axis_index("ctx"), core]).astype(jnp.int32)
    half = lax.dynamic_slice_in_dim(kv_latent.T, core * GROUP, GROUP, 1)
    latents = gather_latent(half)
    recv = lax.all_to_all(pack(q_nope, q_rope, grad_out), "ctx", 0, 0, tiled=True)
    keys, rest = head_call(group_order, place, recv, latents, w_uk, w_uv)
    keys = lax.all_to_all(keys, "ctx", 0, 0, tiled=True)
    keys, rest = lax.optimization_barrier((keys, rest))
    rest = lax.all_to_all(rest, "ctx", 0, 0, tiled=True)
    total = sum_heads(*post(place, keys, w_uk, w_uv))
    peer = lax.ppermute(total, "head", CORE_SWAP)
    low = core == 0
    grad_kv = jnp.concatenate(
        [jnp.where(low, total, peer), jnp.where(low, peer, total)], axis=1
    ).T
    gqn, gqr, guk, guv = finish(rest)
    return gqn, gqr, grad_kv, guk, guv


def solution(mesh):
    in_specs = (
        P("ctx", "head"),
        P("ctx", "head"),
        P("ctx", "head"),
        P("ctx", None),
        P(None, "head"),
        P(None, "head"),
        P(),
    )
    out_specs = (
        P("ctx", "head"),
        P("ctx", "head"),
        P("ctx", None),
        P(None, "head"),
        P(None, "head"),
    )
    return jax.shard_map(
        on_device, mesh=mesh, in_specs=in_specs, out_specs=out_specs, check_vma=False
    )
```

```python
import functools
import math

import jax
import jax.numpy as jnp
from jax import lax
from jax.experimental import pallas as pl
from jax.experimental.pallas import tpu as pltpu
from jax.sharding import PartitionSpec as P

NOPE = 128
ROPE = 64
VHEAD = 128
LATENT = 512
WIDTH = LATENT + ROPE
GROUP = 128
GROUPS = 16
TOKENS = GROUP * GROUPS
CTX = 8
HEAD = 16
MSCALE = 0.1 * math.log(40.0) + 1.0
SCALE = (NOPE + ROPE) ** (-0.5) * MSCALE * MSCALE
BLOCK = 256
BLOCKS = TOKENS // BLOCK
F32 = jnp.float32
BF16 = jnp.bfloat16
VMEM = pl.BlockSpec(memory_space=pltpu.VMEM)
SMEM = pl.BlockSpec(memory_space=pltpu.SMEM)
HBM = pl.BlockSpec(memory_space=pltpu.HBM)
BIG = pltpu.CompilerParams(vmem_limit_bytes=28 * 1024 * 1024)
PARAMS = pltpu.CompilerParams(vmem_limit_bytes=14 * 1024 * 1024)


def near(x):
    return pltpu.with_memory_space_constraint(x, pltpu.VMEM)


def far(x):
    return pltpu.with_memory_space_constraint(x, pltpu.HBM)


def nt(a, b):
    return lax.dot_general(a, b, (((1,), (1,)), ((), ())), preferred_element_type=F32)


def nn(a, b):
    return jnp.dot(a, b, preferred_element_type=F32)


def pack_kernel(q, r, g, send, rope, sems):
    first = pltpu.make_async_copy(r, rope, sems.at[0])
    first.start()
    copies = []
    for i in range(CTX):
        cols = slice(i * 128, (i + 1) * 128)
        copies.append(pltpu.make_async_copy(q.at[:, cols], send.at[i, :256, :], sems.at[1 + 2 * i]))
        copies.append(pltpu.make_async_copy(g.at[:, cols], send.at[i, 256:512, :], sems.at[2 + 2 * i]))
    for copy in copies:
        copy.start()
    first.wait()
    for i in range(CTX):
        part = rope[:, i * ROPE:(i + 1) * ROPE]
        send[i, 512:, :] = jnp.concatenate([part[:128], part[128:]], axis=1)
    for copy in copies:
        copy.wait()


def pack(q, r, g):
    return pl.pallas_call(
        pack_kernel,
        out_shape=jax.ShapeDtypeStruct((CTX, 640, 128), BF16),
        in_specs=[HBM, HBM, HBM],
        out_specs=VMEM,
        scratch_shapes=[pltpu.VMEM((256, CTX * ROPE), BF16), pltpu.SemaphoreType.DMA((17,))],
        compiler_params=PARAMS,
        name="pack",
    )(far(q), far(r), far(g))


def head_kernel(order, place, recv, *refs):
    latents, (uk_all, uv_all, keys, rest) = refs[:6], refs[6:10]
    uk, uv, val, qf, go, kf, kt, vf, gk, gv, gq, grads_w, grads_q, sems = refs[10:]
    column = pl.ds(pl.multiple_of(place[0] * NOPE, NOPE), NOPE)
    uk_copy = pltpu.make_async_copy(uk_all.at[:, column], uk, sems.at[0])
    uv_copy = pltpu.make_async_copy(uv_all.at[:, column], uv, sems.at[1])
    uk_copy.start()
    uv_copy.start()
    me, core = place[0], place[1]
    y, z = me // 2, lax.rem(me, 2)

    def at(s):
        return pl.ds(pl.multiple_of(order[s] * GROUP, GROUP), GROUP)

    for rc in range(2):
        pair, trio, trio_z = latents[rc::2]
        pieces = [(0, 0, pair, 0), (0, 1, pair, 1)]
        for t, dy in enumerate((3, 1, 2)):
            pieces += [(dy, 0, trio, t), (dy, 1, trio_z, t)]
        for dy, rz, src, t in pieces:
            c = lax.rem(y + dy, 4) * 2 + lax.rem(z + rz, 2)
            cols = at(c * 2 + lax.rem(core + rc, 2))
            val[:, cols] = src[t, :LATENT, :]
            kt[NOPE:, cols] = src[t, LATENT:, :]
    for s in range(GROUPS):
        c, b = s // 2, s % 2
        rows = at(s)
        qf[rows, :NOPE] = recv[c, b * 128:(b + 1) * 128, :]
        go[rows, :] = recv[c, 256 + b * 128:256 + (b + 1) * 128, :]
        qf[rows, NOPE:] = recv[c, 512:640, b * ROPE:(b + 1) * ROPE]

    uk_copy.wait()
    uv_copy.wait()
    ukt = jnp.transpose(uk[...].astype(F32)).astype(BF16)
    uvt = jnp.transpose(uv[...].astype(F32)).astype(BF16)
    for p in range(BLOCKS):
        rows = slice(p * BLOCK, (p + 1) * BLOCK)
        latent = val[:, rows]
        k_t = nn(ukt, latent)
        kt[:NOPE, rows] = k_t.astype(BF16)
        kf[rows, :NOPE] = jnp.transpose(k_t).astype(BF16)
        kf[rows, NOPE:] = jnp.transpose(kt[NOPE:, rows].astype(F32)).astype(BF16)
        vf[rows, :] = jnp.transpose(nn(uvt, latent)).astype(BF16)

    factor = SCALE * math.log2(math.e)
    key_at = lax.broadcasted_iota(jnp.int32, (BLOCK, BLOCK), 0)
    query_at = lax.broadcasted_iota(jnp.int32, (BLOCK, BLOCK), 1)
    seen = key_at <= query_at
    def products(i):
        mine = slice(i * BLOCK, (i + 1) * BLOCK)
        scores, grads = [], []
        for j in range(i + 1):
            rows = slice(j * BLOCK, (j + 1) * BLOCK)
            s = nt(kf[rows, :], qf[mine, :]) * factor
            scores.append(jnp.where(seen, s, -jnp.inf) if j == i else s)
            grads.append(nt(vf[rows, :], go[mine, :]))
        return scores, grads

    ahead = products(0)
    for i in range(BLOCKS):
        mine = slice(i * BLOCK, (i + 1) * BLOCK)
        q_i, g_i = qf[mine, :], go[mine, :]
        scores, grads = ahead
        if i + 1 < BLOCKS:
            ahead = products(i + 1)
        top = functools.reduce(jnp.maximum, [jnp.max(s, axis=0, keepdims=True) for s in scores])
        expo = [jnp.exp2(s - top) for s in scores]
        total = functools.reduce(jnp.add, [jnp.sum(e, axis=0, keepdims=True) for e in expo])
        inverse = 1.0 / total
        delta = functools.reduce(
            jnp.add, [jnp.sum(e * d, axis=0, keepdims=True) for e, d in zip(expo, grads)]
        ) * inverse
        acc = None
        for j in range(i + 1):
            rows = slice(j * BLOCK, (j + 1) * BLOCK)
            probs = expo[j] * inverse
            ds = (probs * (grads[j] - delta)).astype(BF16)
            part = nn(kt[:, rows], ds)
            acc = part if acc is None else acc + part
            to_k = nn(ds, q_i)
            to_v = nn(probs.astype(BF16), g_i)
            if j == i:
                gk[rows, :] = to_k
                gv[rows, :] = to_v
            else:
                gk[rows, :] += to_k
                gv[rows, :] += to_v
        gq[mine, :] = jnp.transpose(acc) * SCALE

    gkb = (gk[...] * SCALE).astype(BF16)
    gvb = gv[...].astype(BF16)
    guk = nn(val[...], gkb[:, :NOPE]).astype(BF16)
    guv = nn(val[...], gvb).astype(BF16)
    kf[...] = gkb
    vf[...] = gvb
    grads_w[:LATENT, :] = guk
    grads_w[LATENT:, :] = guv
    copies = [
        pltpu.make_async_copy(grads_w, rest.at[c, 384:, :], sems.at[2 + c]) for c in range(CTX)
    ]
    for c in range(CTX):
        copies[c].start()
        lo, hi = at(2 * c), at(2 * c + 1)
        first, second = gq[lo, :], gq[hi, :]
        grads_q[c, :128, :] = first[:, :NOPE].astype(BF16)
        grads_q[c, 128:256, :] = second[:, :NOPE].astype(BF16)
        grads_q[c, 256:384, :] = jnp.concatenate(
            [first[:, NOPE:], second[:, NOPE:]], axis=1
        ).astype(BF16)
        copies.append(
            pltpu.make_async_copy(grads_q.at[c], rest.at[c, :384, :], sems.at[2 + CTX + c])
        )
        copies[-1].start()
    for c in range(CTX):
        lo, hi = at(2 * c), at(2 * c + 1)
        keys[c, :128, :] = kf[lo, :NOPE]
        keys[c, 128:256, :] = kf[hi, :NOPE]
        keys[c, 256:384, :] = vf[lo, :]
        keys[c, 384:512, :] = vf[hi, :]
        keys[c, 512:, :] = jnp.concatenate([kf[lo, NOPE:], kf[hi, NOPE:]], axis=1)
    for copy in copies:
        copy.wait()


def head_call(order, place, recv, latents, uk, uv):
    return pl.pallas_call(
        head_kernel,
        out_shape=(
            pltpu.VMEM((CTX, 640, 128), BF16),
            pltpu.HBM((CTX, 1408, 128), BF16),
        ),
        in_specs=[SMEM, SMEM] + [VMEM] * 7 + [HBM, HBM],
        out_specs=(VMEM, HBM),
        scratch_shapes=[
            pltpu.VMEM((LATENT, NOPE), BF16),
            pltpu.VMEM((LATENT, VHEAD), BF16),
            pltpu.VMEM((LATENT, TOKENS), BF16),
            pltpu.VMEM((TOKENS, NOPE + ROPE), BF16),
            pltpu.VMEM((TOKENS, VHEAD), BF16),
            pltpu.VMEM((TOKENS, NOPE + ROPE), BF16),
            pltpu.VMEM((NOPE + ROPE, TOKENS), BF16),
            pltpu.VMEM((TOKENS, VHEAD), BF16),
            pltpu.VMEM((TOKENS, NOPE + ROPE), F32),
            pltpu.VMEM((TOKENS, VHEAD), F32),
            pltpu.VMEM((TOKENS, NOPE + ROPE), F32),
            pltpu.VMEM((2 * LATENT, 128), BF16),
            pltpu.VMEM((CTX, 384, 128), BF16),
            pltpu.SemaphoreType.DMA((2 + 2 * CTX,)),
        ],
        compiler_params=BIG,
        name="head",
    )(order, place, near(recv), *[near(x) for x in latents], far(uk), far(uv))


def post_kernel(place, back_all, uk_all, uv_all, own, away, back, uk, uv, sems):
    copies = [
        pltpu.make_async_copy(src, dst, sems.at[k])
        for k, (src, dst) in enumerate(((back_all, back), (uk_all, uk), (uv_all, uv)))
    ]
    for copy in copies:
        copy.start()
    for copy in copies:
        copy.wait()
    acc = rope = None
    for i in range(CTX):
        cols = slice(i * 128, (i + 1) * 128)
        part = nt(uk[:, cols], back[i, :256, :]) + nt(uv[:, cols], back[i, 256:512, :])
        tail = back[i, 512:, :].astype(F32)
        acc = part if acc is None else acc + part
        rope = tail if rope is None else rope + tail
    turned = jnp.transpose(rope)
    low = place[1] == 0
    own[:LATENT, :] = jnp.where(low, acc[:, :128], acc[:, 128:])
    own[LATENT:, :] = jnp.where(low, turned[:ROPE], turned[ROPE:])
    away[:LATENT, :] = jnp.where(low, acc[:, 128:], acc[:, :128]).astype(BF16)
    away[LATENT:, :] = jnp.where(low, turned[ROPE:], turned[:ROPE]).astype(BF16)


def post(place, back, uk, uv):
    return pl.pallas_call(
        post_kernel,
        out_shape=(
            pltpu.VMEM((WIDTH, 128), F32),
            pltpu.VMEM((WIDTH, 128), BF16),
        ),
        in_specs=[SMEM, HBM, HBM, HBM],
        out_specs=(VMEM, VMEM),
        scratch_shapes=[
            pltpu.VMEM((CTX, 640, 128), BF16),
            pltpu.VMEM((LATENT, 1024), BF16),
            pltpu.VMEM((LATENT, 1024), BF16),
            pltpu.SemaphoreType.DMA((3,)),
        ],
        compiler_params=PARAMS,
        name="post",
    )(place, far(back), far(uk), far(uv))


def finish_kernel(rest, gqn, gqr, guk, guv, qn, qr, uk, uv, sems):
    copies = []
    for t in range(CTX):
        cols = slice(128 * t, 128 * (t + 1))
        uk[:, cols] = rest[t, 384:896, :].astype(F32)
        uv[:, cols] = rest[t, 896:, :].astype(F32)
        qn[:, cols] = rest[t, :256, :]
        pair = rest[t, 256:384, :]
        qr[:128, ROPE * t:ROPE * (t + 1)] = pair[:, :ROPE]
        qr[128:, ROPE * t:ROPE * (t + 1)] = pair[:, ROPE:]
        if t % 2 == 1:
            wide = slice(128 * (t - 1), 128 * (t + 1))
            for k, (src, dst) in enumerate(((uk, guk), (uv, guv))):
                copies.append(
                    pltpu.make_async_copy(src.at[:, wide], dst.at[:, wide], sems.at[t // 2 * 2 + k])
                )
                copies[-1].start()
    for k, (src, dst) in enumerate(((qn, gqn), (qr, gqr))):
        copies.append(pltpu.make_async_copy(src, dst, sems.at[8 + k]))
        copies[-1].start()
    for copy in copies:
        copy.wait()


def finish(rest):
    shapes = (((256, 1024), BF16), ((256, 512), BF16), ((LATENT, 1024), F32), ((LATENT, 1024), F32))
    return pl.pallas_call(
        finish_kernel,
        out_shape=tuple(jax.ShapeDtypeStruct(*shape) for shape in shapes),
        in_specs=[VMEM],
        out_specs=(HBM,) * 4,
        scratch_shapes=[pltpu.VMEM(*shape) for shape in shapes] + [pltpu.SemaphoreType.DMA((10,))],
        compiler_params=PARAMS,
        name="finish",
    )(near(rest))


CORE_SWAP = [(i, i ^ 1) for i in range(HEAD)]
ZLO_SWAP = [(i, i ^ 1) for i in range(CTX)]
ZHI_SWAP = [(i, i ^ 8) for i in range(HEAD)]


def from_y(step):
    return [(((c // 2 + step) % 4) * 2 + c % 2, c) for c in range(CTX)]


def from_x(step):
    return [((h & 8) + ((h // 2 + step) % 4) * 2 + h % 2, h) for h in range(HEAD)]


def gather_latent(half, other, trio):
    found = (jnp.stack([half, other]), trio, lax.ppermute(trio, "ctx", ZLO_SWAP))
    return [part for f in found for part in (f, lax.ppermute(f, "head", CORE_SWAP))]


def sum_heads(own, away):
    pair = (own + lax.ppermute(away, "head", CORE_SWAP).astype(F32)).astype(BF16)
    one, two, three = (lax.ppermute(pair, "head", from_x(d)).astype(F32) for d in (1, 2, 3))
    quad = ((pair.astype(F32) + two) + (one + three)).astype(BF16)
    far = lax.ppermute(quad, "head", ZHI_SWAP)
    return (quad.astype(F32) + far.astype(F32)).astype(BF16)


def on_device(q_nope, q_rope, grad_out, kv_latent, w_uk, w_uv, group_order):
    core = lax.axis_index("head") % 2
    place = jnp.stack([lax.axis_index("ctx"), core]).astype(jnp.int32)
    half = lax.dynamic_slice_in_dim(kv_latent.T, core * GROUP, GROUP, 1)
    other = lax.ppermute(half, "ctx", ZLO_SWAP)
    trio = jnp.stack([lax.ppermute(half, "ctx", from_y(d)) for d in (3, 1, 2)])
    packed = pack(q_nope, q_rope, grad_out)
    latents = gather_latent(half, other, trio)
    recv = lax.all_to_all(packed, "ctx", 0, 0, tiled=True)
    keys, rest = head_call(group_order, place, recv, latents, w_uk, w_uv)
    keys = lax.all_to_all(keys, "ctx", 0, 0, tiled=True)
    keys, rest = lax.optimization_barrier((keys, rest))
    rest = lax.all_to_all(rest, "ctx", 0, 0, tiled=True)
    total = sum_heads(*post(place, keys, w_uk, w_uv))
    peer = lax.ppermute(total, "head", CORE_SWAP)
    low = core == 0
    grad_kv = jnp.concatenate(
        [jnp.where(low, total, peer), jnp.where(low, peer, total)], axis=1
    ).T
    gqn, gqr, guk, guv = finish(rest)
    return gqn, gqr, grad_kv, guk, guv


def solution(mesh):
    in_specs = (
        P("ctx", "head"),
        P("ctx", "head"),
        P("ctx", "head"),
        P("ctx", None),
        P(None, "head"),
        P(None, "head"),
        P(),
    )
    out_specs = (
        P("ctx", "head"),
        P("ctx", "head"),
        P("ctx", None),
        P(None, "head"),
        P(None, "head"),
    )
    return jax.shard_map(
        on_device, mesh=mesh, in_specs=in_specs, out_specs=out_specs, check_vma=False
    )
```

```python
import functools
import math

import jax
import jax.numpy as jnp
from jax import lax
from jax.experimental import pallas as pl
from jax.experimental.pallas import tpu as pltpu
from jax.sharding import PartitionSpec as P

NOPE = 128
ROPE = 64
VHEAD = 128
LATENT = 512
WIDTH = LATENT + ROPE
GROUP = 128
GROUPS = 16
TOKENS = GROUP * GROUPS
CTX = 8
HEAD = 16
MSCALE = 0.1 * math.log(40.0) + 1.0
SCALE = (NOPE + ROPE) ** (-0.5) * MSCALE * MSCALE
BLOCK = 256
BLOCKS = TOKENS // BLOCK
F32 = jnp.float32
BF16 = jnp.bfloat16
VMEM = pl.BlockSpec(memory_space=pltpu.VMEM)
SMEM = pl.BlockSpec(memory_space=pltpu.SMEM)
HBM = pl.BlockSpec(memory_space=pltpu.HBM)
BIG = pltpu.CompilerParams(vmem_limit_bytes=34 * 1024 * 1024)
PARAMS = pltpu.CompilerParams(vmem_limit_bytes=14 * 1024 * 1024)


def near(x):
    return pltpu.with_memory_space_constraint(x, pltpu.VMEM)


def far(x):
    return pltpu.with_memory_space_constraint(x, pltpu.HBM)


def nt(a, b):
    return lax.dot_general(a, b, (((1,), (1,)), ((), ())), preferred_element_type=F32)


def nn(a, b):
    return jnp.dot(a, b, preferred_element_type=F32)


def pack_kernel(q, r, g, send, rope, sems):
    first = pltpu.make_async_copy(r, rope, sems.at[0])
    first.start()
    copies = []
    for i in range(CTX):
        cols = slice(i * 128, (i + 1) * 128)
        copies.append(pltpu.make_async_copy(q.at[:, cols], send.at[i, :256, :], sems.at[1 + 2 * i]))
        copies.append(pltpu.make_async_copy(g.at[:, cols], send.at[i, 256:512, :], sems.at[2 + 2 * i]))
    for copy in copies:
        copy.start()
    first.wait()
    for i in range(CTX):
        part = rope[:, i * ROPE:(i + 1) * ROPE]
        send[i, 512:, :] = jnp.concatenate([part[:128], part[128:]], axis=1)
    for copy in copies:
        copy.wait()


def pack(q, r, g):
    return pl.pallas_call(
        pack_kernel,
        out_shape=jax.ShapeDtypeStruct((CTX, 640, 128), BF16),
        in_specs=[HBM, HBM, HBM],
        out_specs=VMEM,
        scratch_shapes=[pltpu.VMEM((256, CTX * ROPE), BF16), pltpu.SemaphoreType.DMA((17,))],
        compiler_params=PARAMS,
        name="pack",
    )(far(q), far(r), far(g))


def head_kernel(order, place, recv, *refs):
    latents, (uk_all, uv_all, keys, rest) = refs[:4], refs[4:8]
    uk, uv, val, qf, go, kf, kt, vf, gk, gv, gq, ds, pb, grads_w, grads_q, sems = refs[8:]
    column = pl.ds(pl.multiple_of(place[0] * NOPE, NOPE), NOPE)
    uk_copy = pltpu.make_async_copy(uk_all.at[:, column], uk, sems.at[0])
    uv_copy = pltpu.make_async_copy(uv_all.at[:, column], uv, sems.at[1])
    uk_copy.start()
    uv_copy.start()
    me, core = place[0], place[1]
    y, z = me // 2, lax.rem(me, 2)

    def at(s):
        return pl.ds(pl.multiple_of(order[s] * GROUP, GROUP), GROUP)

    for rc in range(2):
        quad, quad_z = latents[rc::2]
        pieces = []
        for t, dy in enumerate((0, 3, 1, 2)):
            pieces += [(dy, 0, quad, t), (dy, 1, quad_z, t)]
        for dy, rz, src, t in pieces:
            c = lax.rem(y + dy, 4) * 2 + lax.rem(z + rz, 2)
            cols = at(c * 2 + lax.rem(core + rc, 2))
            val[:, cols] = src[t, :LATENT, :]
            kt[NOPE:, cols] = src[t, LATENT:, :]
    for s in range(GROUPS):
        c, b = s // 2, s % 2
        rows = at(s)
        qf[rows, :NOPE] = recv[c, b * 128:(b + 1) * 128, :]
        go[rows, :] = recv[c, 256 + b * 128:256 + (b + 1) * 128, :]
        qf[rows, NOPE:] = recv[c, 512:640, b * ROPE:(b + 1) * ROPE]

    uk_copy.wait()
    uv_copy.wait()
    ukt = jnp.transpose(uk[...])
    uvt = jnp.transpose(uv[...])
    for p in range(BLOCKS):
        rows = slice(p * BLOCK, (p + 1) * BLOCK)
        latent = val[:, rows]
        k_t = nn(ukt, latent)
        kt[:NOPE, rows] = k_t.astype(BF16)
        kf[rows, :] = jnp.transpose(kt[:, rows])
        vf[rows, :] = jnp.transpose(nn(uvt, latent).astype(BF16))

    factor = SCALE * math.log2(math.e)
    key_at = lax.broadcasted_iota(jnp.int32, (BLOCK, BLOCK), 0)
    query_at = lax.broadcasted_iota(jnp.int32, (BLOCK, BLOCK), 1)
    seen = key_at <= query_at
    def products(i):
        mine, n = slice(i * BLOCK, (i + 1) * BLOCK), (i + 1) * BLOCK
        return nt(kf[:n, :], qf[mine, :]), nt(vf[:n, :], go[mine, :])

    gk[...] = jnp.zeros_like(gk)
    gv[...] = jnp.zeros_like(gv)
    ahead = products(0)
    for i in range(BLOCKS):
        mine, n = slice(i * BLOCK, (i + 1) * BLOCK), (i + 1) * BLOCK
        all_scores, all_grads = ahead
        if i + 1 < BLOCKS:
            ahead = products(i + 1)
        chunks = [slice(j * BLOCK, (j + 1) * BLOCK) for j in range(i + 1)]
        scores = [all_scores[c] * factor for c in chunks]
        scores[i] = jnp.where(seen, scores[i], -jnp.inf)
        grads = [all_grads[c] for c in chunks]
        top = functools.reduce(jnp.maximum, [jnp.max(s, axis=0, keepdims=True) for s in scores])
        expo = [jnp.exp2(s - top) for s in scores]
        total = functools.reduce(jnp.add, [jnp.sum(e, axis=0, keepdims=True) for e in expo])
        inverse = 1.0 / total
        delta = functools.reduce(
            jnp.add, [jnp.sum(e * d, axis=0, keepdims=True) for e, d in zip(expo, grads)]
        ) * inverse
        for c, e, d in zip(chunks, expo, grads):
            probs = e * inverse
            pb[i % 2, c, :] = probs.astype(BF16)
            ds[i % 2, c, :] = (probs * (d - delta)).astype(BF16)
        gk[:n, :] += nn(ds[i % 2, :n, :], qf[mine, :])
        gv[:n, :] += nn(pb[i % 2, :n, :], go[mine, :])
        gq[mine, :] = jnp.transpose(nn(kt[:, :n], ds[i % 2, :n, :])) * SCALE

    gkb = (gk[...] * SCALE).astype(BF16)
    gvb = gv[...].astype(BF16)
    guk = nn(val[...], gkb[:, :NOPE]).astype(BF16)
    guv = nn(val[...], gvb).astype(BF16)
    kf[...] = gkb
    vf[...] = gvb
    grads_w[:LATENT, :] = guk
    grads_w[LATENT:, :] = guv
    copies = [
        pltpu.make_async_copy(grads_w, rest.at[c, 384:, :], sems.at[2 + c]) for c in range(CTX)
    ]
    for c in range(CTX):
        copies[c].start()
        lo, hi = at(2 * c), at(2 * c + 1)
        first, second = gq[lo, :], gq[hi, :]
        grads_q[c, :128, :] = first[:, :NOPE].astype(BF16)
        grads_q[c, 128:256, :] = second[:, :NOPE].astype(BF16)
        grads_q[c, 256:384, :] = jnp.concatenate(
            [first[:, NOPE:], second[:, NOPE:]], axis=1
        ).astype(BF16)
        copies.append(
            pltpu.make_async_copy(grads_q.at[c], rest.at[c, :384, :], sems.at[2 + CTX + c])
        )
        copies[-1].start()
    for c in range(CTX):
        lo, hi = at(2 * c), at(2 * c + 1)
        keys[c, :128, :] = kf[lo, :NOPE]
        keys[c, 128:256, :] = kf[hi, :NOPE]
        keys[c, 256:384, :] = vf[lo, :]
        keys[c, 384:512, :] = vf[hi, :]
        keys[c, 512:, :] = jnp.concatenate([kf[lo, NOPE:], kf[hi, NOPE:]], axis=1)
    for copy in copies:
        copy.wait()


def head_call(order, place, recv, latents, uk, uv):
    return pl.pallas_call(
        head_kernel,
        out_shape=(
            pltpu.VMEM((CTX, 640, 128), BF16),
            pltpu.HBM((CTX, 1408, 128), BF16),
        ),
        in_specs=[SMEM, SMEM] + [VMEM] * 5 + [HBM, HBM],
        out_specs=(VMEM, HBM),
        scratch_shapes=[
            pltpu.VMEM((LATENT, NOPE), BF16),
            pltpu.VMEM((LATENT, VHEAD), BF16),
            pltpu.VMEM((LATENT, TOKENS), BF16),
            pltpu.VMEM((TOKENS, NOPE + ROPE), BF16),
            pltpu.VMEM((TOKENS, VHEAD), BF16),
            pltpu.VMEM((TOKENS, NOPE + ROPE), BF16),
            pltpu.VMEM((NOPE + ROPE, TOKENS), BF16),
            pltpu.VMEM((TOKENS, VHEAD), BF16),
            pltpu.VMEM((TOKENS, NOPE + ROPE), F32),
            pltpu.VMEM((TOKENS, VHEAD), F32),
            pltpu.VMEM((TOKENS, NOPE + ROPE), F32),
            pltpu.VMEM((2, TOKENS, BLOCK), BF16),
            pltpu.VMEM((2, TOKENS, BLOCK), BF16),
            pltpu.VMEM((2 * LATENT, 128), BF16),
            pltpu.VMEM((CTX, 384, 128), BF16),
            pltpu.SemaphoreType.DMA((2 + 2 * CTX,)),
        ],
        compiler_params=BIG,
        name="head",
    )(order, place, near(recv), *[near(x) for x in latents], far(uk), far(uv))


def post_kernel(place, back_all, uk_all, uv_all, own, away, back, uk, uv, sems):
    copies = [
        pltpu.make_async_copy(src, dst, sems.at[k])
        for k, (src, dst) in enumerate(((back_all, back), (uk_all, uk), (uv_all, uv)))
    ]
    for copy in copies:
        copy.start()
    for copy in copies:
        copy.wait()
    acc = rope = None
    for i in range(CTX):
        cols = slice(i * 128, (i + 1) * 128)
        part = nt(uk[:, cols], back[i, :256, :]) + nt(uv[:, cols], back[i, 256:512, :])
        tail = back[i, 512:, :].astype(F32)
        acc = part if acc is None else acc + part
        rope = tail if rope is None else rope + tail
    turned = jnp.transpose(rope)
    low = place[1] == 0
    own[:LATENT, :] = jnp.where(low, acc[:, :128], acc[:, 128:])
    own[LATENT:, :] = jnp.where(low, turned[:ROPE], turned[ROPE:])
    away[:LATENT, :] = jnp.where(low, acc[:, 128:], acc[:, :128]).astype(BF16)
    away[LATENT:, :] = jnp.where(low, turned[ROPE:], turned[:ROPE]).astype(BF16)


def post(place, back, uk, uv):
    return pl.pallas_call(
        post_kernel,
        out_shape=(
            pltpu.VMEM((WIDTH, 128), F32),
            pltpu.VMEM((WIDTH, 128), BF16),
        ),
        in_specs=[SMEM, HBM, HBM, HBM],
        out_specs=(VMEM, VMEM),
        scratch_shapes=[
            pltpu.VMEM((CTX, 640, 128), BF16),
            pltpu.VMEM((LATENT, 1024), BF16),
            pltpu.VMEM((LATENT, 1024), BF16),
            pltpu.SemaphoreType.DMA((3,)),
        ],
        compiler_params=PARAMS,
        name="post",
    )(place, far(back), far(uk), far(uv))


def finish_kernel(rest, gqn, gqr, guk, guv, qn, qr, uk, uv, sems):
    copies = []
    for t in range(CTX):
        cols = slice(128 * t, 128 * (t + 1))
        uk[:, cols] = rest[t, 384:896, :].astype(F32)
        uv[:, cols] = rest[t, 896:, :].astype(F32)
        qn[:, cols] = rest[t, :256, :]
        pair = rest[t, 256:384, :]
        qr[:128, ROPE * t:ROPE * (t + 1)] = pair[:, :ROPE]
        qr[128:, ROPE * t:ROPE * (t + 1)] = pair[:, ROPE:]
        if t % 2 == 1:
            wide = slice(128 * (t - 1), 128 * (t + 1))
            for k, (src, dst) in enumerate(((uk, guk), (uv, guv))):
                copies.append(
                    pltpu.make_async_copy(src.at[:, wide], dst.at[:, wide], sems.at[t // 2 * 2 + k])
                )
                copies[-1].start()
    for k, (src, dst) in enumerate(((qn, gqn), (qr, gqr))):
        copies.append(pltpu.make_async_copy(src, dst, sems.at[8 + k]))
        copies[-1].start()
    for copy in copies:
        copy.wait()


def finish(rest):
    shapes = (((256, 1024), BF16), ((256, 512), BF16), ((LATENT, 1024), F32), ((LATENT, 1024), F32))
    return pl.pallas_call(
        finish_kernel,
        out_shape=tuple(jax.ShapeDtypeStruct(*shape) for shape in shapes),
        in_specs=[VMEM],
        out_specs=(HBM,) * 4,
        scratch_shapes=[pltpu.VMEM(*shape) for shape in shapes] + [pltpu.SemaphoreType.DMA((10,))],
        compiler_params=PARAMS,
        name="finish",
    )(near(rest))


CORE_SWAP = [(i, i ^ 1) for i in range(HEAD)]
ZLO_SWAP = [(i, i ^ 1) for i in range(CTX)]
ZHI_SWAP = [(i, i ^ 8) for i in range(HEAD)]


def from_y(step):
    return [(((c // 2 + step) % 4) * 2 + c % 2, c) for c in range(CTX)]


def from_x(step):
    return [((h & 8) + ((h // 2 + step) % 4) * 2 + h % 2, h) for h in range(HEAD)]


def gather_latent(half, along):
    quad = jnp.stack([half, *along])
    found = (quad, lax.ppermute(quad, "ctx", ZLO_SWAP))
    return [part for f in found for part in (f, lax.ppermute(f, "head", CORE_SWAP))]


def sum_heads(own, away):
    pair = (own + lax.ppermute(away, "head", CORE_SWAP).astype(F32)).astype(BF16)
    one, two, three = (lax.ppermute(pair, "head", from_x(d)).astype(F32) for d in (1, 2, 3))
    quad = ((pair.astype(F32) + two) + (one + three)).astype(BF16)
    far = lax.ppermute(quad, "head", ZHI_SWAP)
    return (quad.astype(F32) + far.astype(F32)).astype(BF16)


def on_device(q_nope, q_rope, grad_out, kv_latent, w_uk, w_uv, group_order):
    core = lax.axis_index("head") % 2
    place = jnp.stack([lax.axis_index("ctx"), core]).astype(jnp.int32)
    half = lax.dynamic_slice_in_dim(kv_latent.T, core * GROUP, GROUP, 1)
    along = [lax.ppermute(half, "ctx", from_y(d)) for d in (3, 1, 2)]
    packed, *along = lax.optimization_barrier((pack(q_nope, q_rope, grad_out), *along))
    latents = gather_latent(half, along)
    recv = lax.all_to_all(packed, "ctx", 0, 0, tiled=True)
    keys, rest = head_call(group_order, place, recv, latents, w_uk, w_uv)
    keys = lax.all_to_all(keys, "ctx", 0, 0, tiled=True)
    keys, rest = lax.optimization_barrier((keys, rest))
    rest = lax.all_to_all(rest, "ctx", 0, 0, tiled=True)
    total = sum_heads(*post(place, keys, w_uk, w_uv))
    peer = lax.ppermute(total, "head", CORE_SWAP)
    low = core == 0
    grad_kv = jnp.concatenate(
        [jnp.where(low, total, peer), jnp.where(low, peer, total)], axis=1
    ).T
    gqn, gqr, guk, guv = finish(rest)
    return gqn, gqr, grad_kv, guk, guv


def solution(mesh):
    in_specs = (
        P("ctx", "head"),
        P("ctx", "head"),
        P("ctx", "head"),
        P("ctx", None),
        P(None, "head"),
        P(None, "head"),
        P(),
    )
    out_specs = (
        P("ctx", "head"),
        P("ctx", "head"),
        P("ctx", None),
        P(None, "head"),
        P(None, "head"),
    )
    return jax.shard_map(
        on_device, mesh=mesh, in_specs=in_specs, out_specs=out_specs, check_vma=False
    )
```

```python
import functools
import math

import jax
import jax.numpy as jnp
from jax import lax
from jax.experimental import pallas as pl
from jax.experimental.pallas import tpu as pltpu
from jax.sharding import PartitionSpec as P

NOPE = 128
ROPE = 64
VHEAD = 128
LATENT = 512
WIDTH = LATENT + ROPE
GROUP = 128
GROUPS = 16
TOKENS = GROUP * GROUPS
CTX = 8
HEAD = 16
MSCALE = 0.1 * math.log(40.0) + 1.0
SCALE = (NOPE + ROPE) ** (-0.5) * MSCALE * MSCALE
BLOCK = 256
BLOCKS = TOKENS // BLOCK
F32 = jnp.float32
BF16 = jnp.bfloat16
VMEM = pl.BlockSpec(memory_space=pltpu.VMEM)
SMEM = pl.BlockSpec(memory_space=pltpu.SMEM)
HBM = pl.BlockSpec(memory_space=pltpu.HBM)
BIG = pltpu.CompilerParams(vmem_limit_bytes=34 * 1024 * 1024)
PARAMS = pltpu.CompilerParams(vmem_limit_bytes=14 * 1024 * 1024)


def near(x):
    return pltpu.with_memory_space_constraint(x, pltpu.VMEM)


def far(x):
    return pltpu.with_memory_space_constraint(x, pltpu.HBM)


def nt(a, b):
    return lax.dot_general(a, b, (((1,), (1,)), ((), ())), preferred_element_type=F32)


def nn(a, b):
    return jnp.dot(a, b, preferred_element_type=F32)


def pack_kernel(q, r, g, send, rope, sems):
    first = pltpu.make_async_copy(r, rope, sems.at[0])
    first.start()
    copies = []
    for i in range(CTX):
        cols = slice(i * 128, (i + 1) * 128)
        copies.append(pltpu.make_async_copy(q.at[:, cols], send.at[i, :256, :], sems.at[1 + 2 * i]))
        copies.append(pltpu.make_async_copy(g.at[:, cols], send.at[i, 256:512, :], sems.at[2 + 2 * i]))
    for copy in copies:
        copy.start()
    first.wait()
    for i in range(CTX):
        part = rope[:, i * ROPE:(i + 1) * ROPE]
        send[i, 512:, :] = jnp.concatenate([part[:128], part[128:]], axis=1)
    for copy in copies:
        copy.wait()


def pack(q, r, g):
    return pl.pallas_call(
        pack_kernel,
        out_shape=jax.ShapeDtypeStruct((CTX, 640, 128), BF16),
        in_specs=[HBM, HBM, HBM],
        out_specs=VMEM,
        scratch_shapes=[pltpu.VMEM((256, CTX * ROPE), BF16), pltpu.SemaphoreType.DMA((17,))],
        compiler_params=PARAMS,
        name="pack",
    )(far(q), far(r), far(g))


def head_kernel(order, place, recv, *refs):
    latents, (uk_all, uv_all, keys, rest) = refs[:8], refs[8:12]
    uk, uv, val, qf, go, kf, kt, vf, gk, gv, gq, ds, pb, grads_w, grads_q, sems = refs[12:]
    column = pl.ds(pl.multiple_of(place[0] * NOPE, NOPE), NOPE)
    uk_copy = pltpu.make_async_copy(uk_all.at[:, column], uk, sems.at[0])
    uv_copy = pltpu.make_async_copy(uv_all.at[:, column], uv, sems.at[1])
    uk_copy.start()
    uv_copy.start()
    me, core = place[0], place[1]
    y, z = me // 2, lax.rem(me, 2)

    def at(s):
        return pl.ds(pl.multiple_of(order[s] * GROUP, GROUP), GROUP)

    for rc in range(2):
        early, below, above, opposite = latents[rc::2]
        pieces = [(dy, rz, early.at[t]) for t, (dy, rz) in enumerate(((0, 0), (3, 0), (1, 0), (2, 0), (0, 1)))]
        pieces += [(3, 1, below), (1, 1, above), (2, 1, opposite)]
        for dy, rz, src in pieces:
            c = lax.rem(y + dy, 4) * 2 + lax.rem(z + rz, 2)
            cols = at(c * 2 + lax.rem(core + rc, 2))
            val[:, cols] = src[:LATENT, :]
            kt[NOPE:, cols] = src[LATENT:, :]
    for s in range(GROUPS):
        c, b = s // 2, s % 2
        rows = at(s)
        qf[rows, :NOPE] = recv[c, b * 128:(b + 1) * 128, :]
        go[rows, :] = recv[c, 256 + b * 128:256 + (b + 1) * 128, :]
        qf[rows, NOPE:] = recv[c, 512:640, b * ROPE:(b + 1) * ROPE]

    uk_copy.wait()
    uv_copy.wait()
    ukt = jnp.transpose(uk[...])
    uvt = jnp.transpose(uv[...])
    for p in range(BLOCKS):
        rows = slice(p * BLOCK, (p + 1) * BLOCK)
        latent = val[:, rows]
        k_t = nn(ukt, latent)
        kt[:NOPE, rows] = k_t.astype(BF16)
        kf[rows, :] = jnp.transpose(kt[:, rows])
        vf[rows, :] = jnp.transpose(nn(uvt, latent).astype(BF16))

    factor = SCALE * math.log2(math.e)
    key_at = lax.broadcasted_iota(jnp.int32, (BLOCK, BLOCK), 0)
    query_at = lax.broadcasted_iota(jnp.int32, (BLOCK, BLOCK), 1)
    seen = key_at <= query_at
    def products(i):
        mine, n = slice(i * BLOCK, (i + 1) * BLOCK), (i + 1) * BLOCK
        return nt(kf[:n, :], qf[mine, :]), nt(vf[:n, :], go[mine, :])

    gk[...] = jnp.zeros_like(gk)
    gv[...] = jnp.zeros_like(gv)
    ahead = products(0)
    for i in range(BLOCKS):
        mine, n = slice(i * BLOCK, (i + 1) * BLOCK), (i + 1) * BLOCK
        all_scores, all_grads = ahead
        if i + 1 < BLOCKS:
            ahead = products(i + 1)
        chunks = [slice(j * BLOCK, (j + 1) * BLOCK) for j in range(i + 1)]
        scores = [all_scores[c] * factor for c in chunks]
        scores[i] = jnp.where(seen, scores[i], -jnp.inf)
        grads = [all_grads[c] for c in chunks]
        top = functools.reduce(jnp.maximum, [jnp.max(s, axis=0, keepdims=True) for s in scores])
        expo = [jnp.exp2(s - top) for s in scores]
        total = functools.reduce(jnp.add, [jnp.sum(e, axis=0, keepdims=True) for e in expo])
        inverse = 1.0 / total
        delta = functools.reduce(
            jnp.add, [jnp.sum(e * d, axis=0, keepdims=True) for e, d in zip(expo, grads)]
        ) * inverse
        for c, e, d in zip(chunks, expo, grads):
            probs = e * inverse
            pb[i % 2, c, :] = probs.astype(BF16)
            ds[i % 2, c, :] = (probs * (d - delta)).astype(BF16)
        gk[:n, :] += nn(ds[i % 2, :n, :], qf[mine, :])
        gv[:n, :] += nn(pb[i % 2, :n, :], go[mine, :])
        gq[mine, :] = jnp.transpose(nn(kt[:, :n], ds[i % 2, :n, :])) * SCALE

    gkb = (gk[...] * SCALE).astype(BF16)
    gvb = gv[...].astype(BF16)
    guk = nn(val[...], gkb[:, :NOPE]).astype(BF16)
    guv = nn(val[...], gvb).astype(BF16)
    kf[...] = gkb
    vf[...] = gvb
    grads_w[:LATENT, :] = guk
    grads_w[LATENT:, :] = guv
    copies = [
        pltpu.make_async_copy(grads_w, rest.at[c, 384:, :], sems.at[2 + c]) for c in range(CTX)
    ]
    for c in range(CTX):
        copies[c].start()
        lo, hi = at(2 * c), at(2 * c + 1)
        first, second = gq[lo, :], gq[hi, :]
        grads_q[c, :128, :] = first[:, :NOPE].astype(BF16)
        grads_q[c, 128:256, :] = second[:, :NOPE].astype(BF16)
        grads_q[c, 256:384, :] = jnp.concatenate(
            [first[:, NOPE:], second[:, NOPE:]], axis=1
        ).astype(BF16)
        copies.append(
            pltpu.make_async_copy(grads_q.at[c], rest.at[c, :384, :], sems.at[2 + CTX + c])
        )
        copies[-1].start()
    for c in range(CTX):
        lo, hi = at(2 * c), at(2 * c + 1)
        keys[c, :128, :] = kf[lo, :NOPE]
        keys[c, 128:256, :] = kf[hi, :NOPE]
        keys[c, 256:384, :] = vf[lo, :]
        keys[c, 384:512, :] = vf[hi, :]
        keys[c, 512:, :] = jnp.concatenate([kf[lo, NOPE:], kf[hi, NOPE:]], axis=1)
    for copy in copies:
        copy.wait()


def head_call(order, place, recv, latents, uk, uv):
    return pl.pallas_call(
        head_kernel,
        out_shape=(
            pltpu.VMEM((CTX, 640, 128), BF16),
            pltpu.HBM((CTX, 1408, 128), BF16),
        ),
        in_specs=[SMEM, SMEM] + [VMEM] * 9 + [HBM, HBM],
        out_specs=(VMEM, HBM),
        scratch_shapes=[
            pltpu.VMEM((LATENT, NOPE), BF16),
            pltpu.VMEM((LATENT, VHEAD), BF16),
            pltpu.VMEM((LATENT, TOKENS), BF16),
            pltpu.VMEM((TOKENS, NOPE + ROPE), BF16),
            pltpu.VMEM((TOKENS, VHEAD), BF16),
            pltpu.VMEM((TOKENS, NOPE + ROPE), BF16),
            pltpu.VMEM((NOPE + ROPE, TOKENS), BF16),
            pltpu.VMEM((TOKENS, VHEAD), BF16),
            pltpu.VMEM((TOKENS, NOPE + ROPE), F32),
            pltpu.VMEM((TOKENS, VHEAD), F32),
            pltpu.VMEM((TOKENS, NOPE + ROPE), F32),
            pltpu.VMEM((2, TOKENS, BLOCK), BF16),
            pltpu.VMEM((2, TOKENS, BLOCK), BF16),
            pltpu.VMEM((2 * LATENT, 128), BF16),
            pltpu.VMEM((CTX, 384, 128), BF16),
            pltpu.SemaphoreType.DMA((2 + 2 * CTX,)),
        ],
        compiler_params=BIG,
        name="head",
    )(order, place, near(recv), *[near(x) for x in latents], far(uk), far(uv))


def post_kernel(place, back_all, uk_all, uv_all, own, away, back, uk, uv, sems):
    copies = [
        pltpu.make_async_copy(src, dst, sems.at[k])
        for k, (src, dst) in enumerate(((back_all, back), (uk_all, uk), (uv_all, uv)))
    ]
    for copy in copies:
        copy.start()
    for copy in copies:
        copy.wait()
    acc = rope = None
    for i in range(CTX):
        cols = slice(i * 128, (i + 1) * 128)
        part = nt(uk[:, cols], back[i, :256, :]) + nt(uv[:, cols], back[i, 256:512, :])
        tail = back[i, 512:, :].astype(F32)
        acc = part if acc is None else acc + part
        rope = tail if rope is None else rope + tail
    turned = jnp.transpose(rope)
    low = place[1] == 0
    own[:LATENT, :] = jnp.where(low, acc[:, :128], acc[:, 128:])
    own[LATENT:, :] = jnp.where(low, turned[:ROPE], turned[ROPE:])
    away[:LATENT, :] = jnp.where(low, acc[:, 128:], acc[:, :128]).astype(BF16)
    away[LATENT:, :] = jnp.where(low, turned[ROPE:], turned[:ROPE]).astype(BF16)


def post(place, back, uk, uv):
    return pl.pallas_call(
        post_kernel,
        out_shape=(
            pltpu.VMEM((WIDTH, 128), F32),
            pltpu.VMEM((WIDTH, 128), BF16),
        ),
        in_specs=[SMEM, HBM, HBM, HBM],
        out_specs=(VMEM, VMEM),
        scratch_shapes=[
            pltpu.VMEM((CTX, 640, 128), BF16),
            pltpu.VMEM((LATENT, 1024), BF16),
            pltpu.VMEM((LATENT, 1024), BF16),
            pltpu.SemaphoreType.DMA((3,)),
        ],
        compiler_params=PARAMS,
        name="post",
    )(place, far(back), far(uk), far(uv))


def finish_kernel(rest, gqn, gqr, guk, guv, qn, qr, uk, uv, sems):
    copies = []
    for t in range(CTX):
        cols = slice(128 * t, 128 * (t + 1))
        uk[:, cols] = rest[t, 384:896, :].astype(F32)
        uv[:, cols] = rest[t, 896:, :].astype(F32)
        qn[:, cols] = rest[t, :256, :]
        pair = rest[t, 256:384, :]
        qr[:128, ROPE * t:ROPE * (t + 1)] = pair[:, :ROPE]
        qr[128:, ROPE * t:ROPE * (t + 1)] = pair[:, ROPE:]
        if t % 2 == 1:
            wide = slice(128 * (t - 1), 128 * (t + 1))
            for k, (src, dst) in enumerate(((uk, guk), (uv, guv))):
                copies.append(
                    pltpu.make_async_copy(src.at[:, wide], dst.at[:, wide], sems.at[t // 2 * 2 + k])
                )
                copies[-1].start()
    for k, (src, dst) in enumerate(((qn, gqn), (qr, gqr))):
        copies.append(pltpu.make_async_copy(src, dst, sems.at[8 + k]))
        copies[-1].start()
    for copy in copies:
        copy.wait()


def finish(rest):
    shapes = (((256, 1024), BF16), ((256, 512), BF16), ((LATENT, 1024), F32), ((LATENT, 1024), F32))
    return pl.pallas_call(
        finish_kernel,
        out_shape=tuple(jax.ShapeDtypeStruct(*shape) for shape in shapes),
        in_specs=[VMEM],
        out_specs=(HBM,) * 4,
        scratch_shapes=[pltpu.VMEM(*shape) for shape in shapes] + [pltpu.SemaphoreType.DMA((10,))],
        compiler_params=PARAMS,
        name="finish",
    )(near(rest))


CORE_SWAP = [(i, i ^ 1) for i in range(HEAD)]
ZLO_SWAP = [(i, i ^ 1) for i in range(CTX)]
ZHI_SWAP = [(i, i ^ 8) for i in range(HEAD)]


def from_y(step):
    return [(((c // 2 + step) % 4) * 2 + c % 2, c) for c in range(CTX)]


def from_x(step):
    return [((h & 8) + ((h // 2 + step) % 4) * 2 + h % 2, h) for h in range(HEAD)]


def gather_latent(half, below, above, far_off, other):
    found = [jnp.stack([half, below, above, far_off, other])]
    found += [lax.ppermute(other, "ctx", from_y(d)) for d in (3, 1)]
    found.append(lax.ppermute(far_off, "ctx", ZLO_SWAP))
    return [part for f in found for part in (f, lax.ppermute(f, "head", CORE_SWAP))]


def sum_heads(own, away):
    pair = (own + lax.ppermute(away, "head", CORE_SWAP).astype(F32)).astype(BF16)
    one, two, three = (lax.ppermute(pair, "head", from_x(d)).astype(F32) for d in (1, 2, 3))
    quad = ((pair.astype(F32) + two) + (one + three)).astype(BF16)
    far = lax.ppermute(quad, "head", ZHI_SWAP)
    return (quad.astype(F32) + far.astype(F32)).astype(BF16)


def on_device(q_nope, q_rope, grad_out, kv_latent, w_uk, w_uv, group_order):
    core = lax.axis_index("head") % 2
    place = jnp.stack([lax.axis_index("ctx"), core]).astype(jnp.int32)
    half = lax.dynamic_slice_in_dim(kv_latent.T, core * GROUP, GROUP, 1)
    blocks = [half] + [lax.ppermute(half, "ctx", from_y(d)) for d in (3, 1, 2)]
    blocks.append(lax.ppermute(half, "ctx", ZLO_SWAP))
    packed, *blocks = lax.optimization_barrier((pack(q_nope, q_rope, grad_out), *blocks))
    latents = gather_latent(*blocks)
    recv = lax.all_to_all(packed, "ctx", 0, 0, tiled=True)
    keys, rest = head_call(group_order, place, recv, latents, w_uk, w_uv)
    keys = lax.all_to_all(keys, "ctx", 0, 0, tiled=True)
    keys, rest = lax.optimization_barrier((keys, rest))
    rest = lax.all_to_all(rest, "ctx", 0, 0, tiled=True)
    total = sum_heads(*post(place, keys, w_uk, w_uv))
    peer = lax.ppermute(total, "head", CORE_SWAP)
    low = core == 0
    grad_kv = jnp.concatenate(
        [jnp.where(low, total, peer), jnp.where(low, peer, total)], axis=1
    ).T
    gqn, gqr, guk, guv = finish(rest)
    return gqn, gqr, grad_kv, guk, guv


def solution(mesh):
    in_specs = (
        P("ctx", "head"),
        P("ctx", "head"),
        P("ctx", "head"),
        P("ctx", None),
        P(None, "head"),
        P(None, "head"),
        P(),
    )
    out_specs = (
        P("ctx", "head"),
        P("ctx", "head"),
        P("ctx", None),
        P(None, "head"),
        P(None, "head"),
    )
    return jax.shard_map(
        on_device, mesh=mesh, in_specs=in_specs, out_specs=out_specs, check_vma=False
    )
```
